32 devices in a mesh: groups: 2 (over y), mp: 4 (over z), inner: 2 (over x), hst: 2 (over core).
Axes of the slice: x: 2, y: 2, z: 4, core: 2. Of those that a mesh axis runs over, the one named last changes fastest.
Arguments:
- tokens: bfloat16 [256, 8192], P(('groups', 'inner', 'hst'), 'mp'), parts along dimension 0, may hold values from -6 to 6
- query_weight: bfloat16 [8192, 8192], P('mp', 'inner'), may hold values from -0.0625 to 0.0625
- key_weight: bfloat16 [8192, 1024], P('mp', 'inner'), may hold values from -0.0625 to 0.0625
- value_weight: bfloat16 [8192, 1024], P('mp', 'inner'), may hold values from -0.0625 to 0.0625
- adapter_down_weight: bfloat16 [32, 8192, 128], P(('groups', 'mp', 'inner', 'hst')), parts along dimension 0, may hold values from -0.0625 to 0.0625
- adapter_up_weight: bfloat16 [32, 128, 1024], P(('groups', 'mp', 'inner', 'hst')), parts along dimension 0, may hold values from -0.75 to 0.75
- adapter_rank: int32 [32], P(('groups', 'mp', 'inner', 'hst')), parts along dimension 0, may hold values from 16 to 128
- row_adapter_index: int32 [256, 1], P('groups'), parts along dimension 0, may hold values from 0 to 7; in each aligned block of 32 rows (0 to 31, 32 to 63, ...) at most 8 rows name the same one
- owner_device_map: int32 [16], P('groups'), parts along dimension 0, may hold values from 0 to 7, each once
- lengths: int32 [256], P('groups'), parts along dimension 0, may hold values from 1 to 64
- page_holder_index: int32 [256, 8, 4], P('groups', 'inner'), parts along dimension 0, may hold values from 0 to 3, as said below
- page_pool_slot: int32 [256, 8, 4], P('groups', 'inner'), parts along dimension 0, may hold values from 0 to 63, as said below
- key_value_pool: bfloat16 [8, 8, 2, 64, 16, 256], P(('groups', 'mp'), 'inner', 'hst'), parts along dimension 0, may hold values from -500 to 500
Outputs:
- attended: bfloat16 [4, 64, 8192], P(('groups', 'hst'), 'mp', 'inner'), parts along dimension 0
- new_kv: bfloat16 [4, 64, 2048], P(('groups', 'hst'), 'mp', 'inner'), parts along dimension 0
The draws below stay inside these ranges and needn't reach their ends.
There are 2 independent parts, one for each index of `groups`. The reference program is written for one: setup_inputs(seed, part) draws one part's arguments, and reference() takes and returns one part's arrays. A program takes and returns all parts, laid end to end along the dimension named above; an argument that names none is the same for every part. Nothing has to cross between parts.
Inputs may be any that keep to these rules, and one draw needn't show every extreme that they name: `row_adapter_index`: among the 32 rows of one input device (aligned blocks of 32 rows) no adapter is named by more than 8 rows. `owner_device_map`: each owner device index once. `page_holder_index`: for each index of hst and key-value head, every (holder, slot) holds exactly one page. Take the rows of one side in side order, in blocks of 16: the pages of one block and one key-value head lie on each holder 16 - 1 or 16 + 3 times, and 19 is reached by some holder of every block. `page_pool_slot`: slot of the page in the pool of its holder, key-value head and index of hst.
All inputs are finite; a program needn't handle non-finite values.
Results may differ from the reference program's by a relative error of at most 0.012.
The reference program's roundings to bfloat16 on the way count: a program that leaves them out, or rounds other values in their place, can miss the bound.
Values may be sent and summed in bfloat16 or wider, within the bound.
A program may use at most 128 MiB of HBM per device.

```python
import math
import jax
import jax.numpy as jnp
import numpy as np
from jax import lax

MODEL_WIDTH = 8192
H = 64
KEY_VALUE_HEADS = 8
HEAD_WIDTH = 128
PADDED_RANK = 128
DEVICE_ROWS = 32
NPAGE = 4
PAGE = 16
ROWS = 128
ROWS_SIDE = 64
RB = 16
CTX = 64
ADAPT_SIDE = 8
ADAPTER_TOTAL = 16
CAP = 8
BASE = 16
SLOTS = 64
N_MP = 4
N_INNER = 2
N_HST = 2


def shuffled_rows(key, count, length):
    return jax.vmap(jax.random.permutation, in_axes=(0, None))(jax.random.split(key, count), length)


def group_tables(group_key):
    first_key, second_key, third_key, fourth_key = jax.random.split(group_key, 4)
    block_order = jax.random.permutation(first_key, N_MP)
    holder_order = jax.random.permutation(second_key, N_MP)
    turn_index = (block_order[:, None] + holder_order[None, :]) % N_MP
    counts = jnp.where(turn_index % 4 == 0, BASE + 3, BASE - 1).astype(jnp.int32)
    upper_bound = jnp.cumsum(counts, axis=1)
    lower_bound = upper_bound - counts
    before = jnp.cumsum(counts, axis=0) - counts
    entries = RB * NPAGE
    page_order = shuffled_rows(third_key, N_MP, entries).astype(jnp.int32)
    holder = jnp.sum((page_order[:, :, None] >= upper_bound[:, None, :]).astype(jnp.int32), axis=2)
    start_index = jnp.take_along_axis(lower_bound, holder, axis=1)
    offset = jnp.take_along_axis(before, holder, axis=1) + page_order - start_index
    shuffle = shuffled_rows(fourth_key, N_MP, SLOTS).astype(jnp.int32)
    slot_index = shuffle[holder, offset]
    return (holder, slot_index)


def page_tables(key):
    base_key = jax.random.fold_in(key, 11)
    group_keys = jax.random.split(base_key, N_HST * KEY_VALUE_HEADS)
    holder, slot_index = jax.vmap(group_tables)(group_keys)

    def arrange(table):
        shaped = table.reshape(N_HST, KEY_VALUE_HEADS, N_INNER, DEVICE_ROWS, NPAGE)
        return jnp.transpose(shaped, (2, 0, 3, 1, 4)).reshape(ROWS, KEY_VALUE_HEADS, NPAGE).astype(jnp.int32)
    return (arrange(holder), arrange(slot_index))


def draw_page_holder_index(key, part):
    return page_tables(key)[0]


def draw_page_pool_slot(key, part):
    return page_tables(key)[1]


def draw_key_value_pool(key, part):
    key = jax.random.fold_in(key, 3)
    normal_key = jax.random.fold_in(key, 0)
    pool_shape = (N_MP, KEY_VALUE_HEADS, N_HST, SLOTS, PAGE, 2 * HEAD_WIDTH)
    values = jnp.clip(jax.random.normal(normal_key, pool_shape, jnp.float32), -5.0, 5.0)
    return values.astype(jnp.bfloat16)


def with_ends(drawn, stream_key, least, high):
    longest = drawn.shape.index(max(drawn.shape))
    spots = []
    for shift in (0, 1):
        where = [jax.random.randint(jax.random.fold_in(stream_key, axis), (), 0, length) for axis, length in enumerate(drawn.shape)]
        where[longest] = (where[longest] + shift) % drawn.shape[longest]
        spots.append(tuple(where))
    return drawn.at[spots[0]].set(least).at[spots[1]].set(high)


def block_levels(own_key, dims, pieces, least, largest):
    def one(position, blocks):
        heights = jax.random.uniform(jax.random.fold_in(jax.random.fold_in(own_key, 6), position), (blocks,), jnp.float32, least / len(pieces), largest / len(pieces))
        return jnp.repeat(jnp.exp(heights), dims[position] // blocks).reshape((-1,) + (1,) * (len(dims) - position - 1))

    gain = one(*pieces[0])
    for cut in pieces[1:]:
        gain = gain * one(*cut)
    return gain


def assign_block(key, own, number, rows, count, top, reach, lean):
    sequence = jax.random.permutation(key, count)
    heavy_load, ordinary = portions_of(count, rows * top, reach, lean, True), portions_of(count, rows * top, reach, lean, False)
    places = jnp.arange(count)

    def named(sizes, offset_by):
        used = int((sizes > 0).sum())
        fixed = max(1, used // 4)
        shifted = fixed + (places - fixed + offset_by * (used - fixed)) % max(1, count - fixed)
        return jnp.zeros((count,), jnp.int32).at[sequence[jnp.where(places < fixed, places, shifted)]].set(jnp.asarray(sizes, jnp.int32))

    sizes = jnp.where(number % 4 == 0, named(heavy_load, number // 4), named(ordinary, number - number // 4 - 1))
    mixed = jax.random.permutation(jax.random.fold_in(own, 3), count)
    source_of, receiver = mixed[0:count // 2 * 2:2], mixed[1:count // 2 * 2:2]
    room = jnp.minimum(sizes[source_of] - 1, reach - sizes[receiver]) // 2
    room = jnp.where((source_of == sequence[0]) | (receiver == sequence[0]) | (sizes[receiver] == 0), 0, jnp.maximum(room, 0))
    shifted = jax.random.randint(jax.random.fold_in(own, 4), (count // 2,), 0, 1 << 20) % (room + 1)
    sizes = sizes.at[source_of].add(-shifted).at[receiver].add(shifted)
    members = jnp.searchsorted(jnp.cumsum(sizes), jnp.arange(rows * top), side="right").astype(jnp.int32)
    table = members.reshape(top, rows).T
    table = table[jax.random.permutation(jax.random.fold_in(own, 1), rows)]
    offset_by = jax.random.randint(jax.random.fold_in(own, 2), (rows, 1), 0, top)
    return jnp.take_along_axis(table, (jnp.arange(top)[None, :] + offset_by) % top, axis=1)


def portions_of(number_of, total, reach, slope, full):
    weights = [(1 << 20) // math.isqrt(grade ** slope) + 1 for grade in range(1, number_of + 1)]
    largest = reach if full else min(reach, max(-(-total // number_of), total * weights[0] // sum(weights)))
    least = 1 if total - largest >= number_of - 1 else 0
    given, spare = [largest] + [least] * (number_of - 1), total - largest - least * (number_of - 1)
    while spare > 0:
        free = [i for i in range(1, number_of) if given[i] < largest] or [i for i in range(1, number_of) if given[i] < reach]
        pool, remaining = sum([weights[i] for i in free]), spare
        for i in free:
            extra = min(reach - given[i], max(1, remaining * weights[i] // pool), spare)
            given[i] = given[i] + extra
            spare = spare - extra
    return np.array(given)


def gaussian(key, extent, width, limit, cuts=(), kind=jnp.bfloat16):
    gain = block_levels(key, extent, cuts, -0.22, 0.18) if cuts else 1.0
    values = jax.random.normal(key, extent, jnp.float32) * width * gain
    return jnp.minimum(jnp.maximum(values, -limit), limit).astype(kind)


def setup_inputs(seed: int = 0, part: int = 0) -> dict:
    key_of = jax.random.split(jax.random.key(seed), 14)
    own_keys = jax.random.split(jax.random.fold_in(key_of[13], part), 14)
    tokens = gaussian(own_keys[0], (ROWS, MODEL_WIDTH), 1.0, 6.0, ((0, 4), (1, 4)))
    query_weight = gaussian(key_of[1], (MODEL_WIDTH, H * HEAD_WIDTH), MODEL_WIDTH ** -0.5, 0.0625, ((0, 4), (1, 2)))
    key_weight = gaussian(key_of[2], (MODEL_WIDTH, KEY_VALUE_HEADS * HEAD_WIDTH), MODEL_WIDTH ** -0.5, 0.0625, ((0, 4), (1, 2)))
    value_weight = gaussian(key_of[3], (MODEL_WIDTH, KEY_VALUE_HEADS * HEAD_WIDTH), MODEL_WIDTH ** -0.5, 0.0625, ((0, 4), (1, 2)))
    adapter_down_weight = gaussian(own_keys[4], (ADAPTER_TOTAL, MODEL_WIDTH, PADDED_RANK), MODEL_WIDTH ** -0.5, 0.0625, ((0, 16),))
    adapter_up_weight = gaussian(own_keys[5], (ADAPTER_TOTAL, PADDED_RANK, KEY_VALUE_HEADS * HEAD_WIDTH), (PADDED_RANK // 2) ** -0.5, 0.75, ((0, 16),))
    adapter_rank = with_ends(jax.random.randint(own_keys[6], (ADAPTER_TOTAL,), PADDED_RANK // 8, PADDED_RANK + 1), jax.random.fold_in(own_keys[6], 1), PADDED_RANK // 8, PADDED_RANK).astype(jnp.int32)
    row_adapter_index_keys = jax.random.split(jax.random.fold_in(own_keys[7], 1), ROWS // DEVICE_ROWS)
    row_adapter_index_turns = jax.random.permutation(jax.random.fold_in(own_keys[7], 3), ROWS // DEVICE_ROWS)
    row_adapter_index = jax.vmap(lambda own, number: assign_block(jax.random.fold_in(own_keys[7], 2), own, number, DEVICE_ROWS, ADAPT_SIDE, 1, CAP, 2))(row_adapter_index_keys, row_adapter_index_turns).reshape((ROWS, 1))
    owner_device_map = jax.random.permutation(own_keys[8], ADAPT_SIDE).astype(jnp.int32)
    lengths = with_ends(jax.random.randint(own_keys[9], (ROWS,), 1, CTX + 1), jax.random.fold_in(own_keys[9], 1), 1, CTX).astype(jnp.int32)
    page_holder_index = draw_page_holder_index(jax.random.fold_in(jax.random.fold_in(key_of[13], part), 71), part)
    page_pool_slot = draw_page_pool_slot(jax.random.fold_in(jax.random.fold_in(key_of[13], part), 71), part)
    key_value_pool = draw_key_value_pool(jax.random.fold_in(jax.random.fold_in(key_of[13], part), 71), part)
    return {"tokens": tokens, "query_weight": query_weight, "key_weight": key_weight, "value_weight": value_weight, "adapter_down_weight": adapter_down_weight, "adapter_up_weight": adapter_up_weight, "adapter_rank": adapter_rank, "row_adapter_index": row_adapter_index, "owner_device_map": owner_device_map, "lengths": lengths, "page_holder_index": page_holder_index, "page_pool_slot": page_pool_slot, "key_value_pool": key_value_pool}


THETA = 500000.0


def to_sides(values):
    shaped = values.reshape((N_INNER, N_HST, DEVICE_ROWS) + values.shape[1:])
    moved = jnp.moveaxis(shaped, 1, 0)
    return moved.reshape((N_HST, N_INNER * DEVICE_ROWS) + values.shape[1:])


def rotate(values, rope_angle):
    half_width = values.shape[-1] // 2
    first_half = values[..., :half_width]
    second_half = values[..., half_width:]
    cosine = jnp.cos(rope_angle)
    sine_part = jnp.sin(rope_angle)
    return jnp.concatenate([first_half * cosine - second_half * sine_part, second_half * cosine + first_half * sine_part], axis=-1)


def reference(tokens, query_weight, key_weight, value_weight, adapter_down_weight, adapter_up_weight, adapter_rank, row_adapter_index, owner_device_map, lengths, page_holder_index, page_pool_slot, key_value_pool):
    proj_query = jnp.dot(tokens, query_weight, preferred_element_type=jnp.float32)
    proj_key = jnp.dot(tokens, key_weight, preferred_element_type=jnp.float32)
    proj_value = jnp.dot(tokens, value_weight, preferred_element_type=jnp.float32)
    side_of_row = ((jnp.arange(ROWS) // DEVICE_ROWS) % N_HST).astype(jnp.int32)
    owner_slot_index = (owner_device_map[row_adapter_index[:, 0]] * N_HST + side_of_row).astype(jnp.int32)

    def adapter_block(block_arguments):
        block_rows, block_slot_list = block_arguments
        down_matrices = adapter_down_weight[block_slot_list].astype(jnp.float32)
        reduced_rows = jnp.einsum('bd,bdr->br', block_rows.astype(jnp.float32), down_matrices)
        rank_ceiling = adapter_rank[block_slot_list]
        kept_cols = jnp.arange(PADDED_RANK)[None, :] < rank_ceiling[:, None]
        factor = PADDED_RANK / (8.0 * rank_ceiling.astype(jnp.float32))
        reduced_rows = jnp.where(kept_cols, reduced_rows * factor[:, None], 0.0)
        reduced_rows = lax.optimization_barrier(reduced_rows.astype(jnp.bfloat16)).astype(jnp.float32)
        up_matrices = adapter_up_weight[block_slot_list].astype(jnp.float32)
        return jnp.einsum('br,brc->bc', reduced_rows, up_matrices).astype(jnp.bfloat16)

    home_devices = N_INNER * N_HST
    delta_values = lax.map(adapter_block, (tokens.reshape(home_devices, DEVICE_ROWS, MODEL_WIDTH), owner_slot_index.reshape(home_devices, DEVICE_ROWS)))
    delta_values = lax.optimization_barrier(delta_values.reshape(ROWS, KEY_VALUE_HEADS * HEAD_WIDTH)).astype(jnp.float32)
    value_sum = proj_value + delta_values

    half_width = HEAD_WIDTH // 2
    inv_freq = THETA ** (-(2.0 * jnp.arange(half_width, dtype=jnp.float32)) / HEAD_WIDTH)
    rope_angle = lengths.astype(jnp.float32)[:, None, None] * inv_freq
    query = rotate(proj_query.reshape(ROWS, H, HEAD_WIDTH), rope_angle).astype(jnp.bfloat16)
    key_new = rotate(proj_key.reshape(ROWS, KEY_VALUE_HEADS, HEAD_WIDTH), rope_angle).astype(jnp.bfloat16)
    fresh_value = value_sum.reshape(ROWS, KEY_VALUE_HEADS, HEAD_WIDTH).astype(jnp.bfloat16)
    query = lax.optimization_barrier(query)
    key_new = lax.optimization_barrier(key_new)
    fresh_value = lax.optimization_barrier(fresh_value)
    new_kv = to_sides(jnp.concatenate([key_new, fresh_value], axis=2).reshape(ROWS, KEY_VALUE_HEADS * 2 * HEAD_WIDTH))

    group_size = H // KEY_VALUE_HEADS
    query_side = to_sides(query).reshape(N_HST, ROWS_SIDE, KEY_VALUE_HEADS, group_size, HEAD_WIDTH)
    key_side = to_sides(key_new)
    value_side = to_sides(fresh_value)
    holder_side = to_sides(page_holder_index)
    slot_side = to_sides(page_pool_slot)
    length_side = to_sides(lengths)
    side_grid = jnp.arange(N_HST, dtype=jnp.int32)[:, None, None]
    valid_tokens = jnp.arange(CTX)[None, None, :] < length_side[:, :, None]
    score_scale = HEAD_WIDTH ** -0.5

    def attend_head(head_index):
        holder_rows = jnp.take(holder_side, head_index, axis=2)
        slot_rows = jnp.take(slot_side, head_index, axis=2)
        page_rows = key_value_pool[holder_rows, head_index, side_grid, slot_rows]
        page_rows = page_rows.reshape(N_HST, ROWS_SIDE, CTX, 2 * HEAD_WIDTH).astype(jnp.float32)
        query_head = jnp.take(query_side, head_index, axis=2).astype(jnp.float32)
        key_head = jnp.take(key_side, head_index, axis=2).astype(jnp.float32)
        value_head = jnp.take(value_side, head_index, axis=2).astype(jnp.float32)
        cache_score = jnp.einsum('srgd,srtd->srgt', query_head, page_rows[..., :HEAD_WIDTH]) * score_scale
        new_score = jnp.einsum('srgd,srd->srg', query_head, key_head) * score_scale
        masked = jnp.where(valid_tokens[:, :, None, :], cache_score, -jnp.inf)
        row_top = jnp.maximum(jnp.max(masked, axis=3), new_score)
        cache_weight = jnp.exp(masked - row_top[..., None])
        new_weight = jnp.exp(new_score - row_top)
        weight_total = jnp.sum(cache_weight, axis=3) + new_weight
        cache_share = lax.optimization_barrier((cache_weight / weight_total[..., None]).astype(jnp.bfloat16)).astype(jnp.float32)
        fresh_share = lax.optimization_barrier((new_weight / weight_total).astype(jnp.bfloat16)).astype(jnp.float32)
        mixed = jnp.einsum('srgt,srtd->srgd', cache_share, page_rows[..., HEAD_WIDTH:]) + fresh_share[..., None] * value_head[:, :, None, :]
        return mixed.astype(jnp.bfloat16)

    attended = lax.map(attend_head, jnp.arange(KEY_VALUE_HEADS, dtype=jnp.int32))
    attended = jnp.moveaxis(attended, 0, 2).reshape(N_HST, ROWS_SIDE, H * HEAD_WIDTH)
    return attended, new_kv
```

```python
import functools

import jax
import jax.numpy as jnp
from jax import lax
from jax.experimental import pallas as pl
from jax.experimental.pallas import tpu as pltpu
from jax.sharding import PartitionSpec as P

HEAD_WIDTH = 128
NPAGE = 4
PAGE = 16
THETA = 500000.0
MESH = pl.DeviceIdType.MESH
PARTIAL = jnp.float32
BACK = jnp.bfloat16


def kernel(
    dims,
    tokens,
    wq,
    wk,
    wv,
    down,
    up,
    rank,
    table,
    omap,
    rope,
    pool,
    attended,
    new_kv,
    x_all,
    lo,
    lr,
    wq_v,
    wk_v,
    wv_v,
    down_v,
    up_v,
    pool_v,
    part,
    rs_in,
    partkv,
    rskv,
    q_all,
    bias,
    s_buf,
    p_buf,
    ao,
    st,
    ain,
    sin,
    dl_out,
    dl_in,
    rot,
    local_sem,
    x_send,
    x_recv,
    l_send,
    l_recv,
    d_send,
    d_recv,
    kv_send,
    kv_recv,
    r_send,
    r_recv,
    q_send,
    q_recv,
    a_send,
    a_recv,
    t_send,
    t_recv,
):
    MP, IN, SD = dims
    m = lax.axis_index("mp")
    i = lax.axis_index("inner")
    h = lax.axis_index("hst")
    R, W = tokens.shape
    RS = R * IN
    B = RS // MP
    K, _, QW = wq_v.shape
    KC = wk_v.shape[1]
    G = QW // HEAD_WIDTH
    SLOTS = pool_v.shape[1]
    T = SLOTS * PAGE
    OC = MP * IN
    CAP = max(2, 2 * R // OC)
    L = IN * CAP
    f32 = jnp.float32
    bf16 = jnp.bfloat16
    scale = HEAD_WIDTH ** (-0.5)

    def peer_of(d):
        return lax.rem(m + d, MP)

    def source_of(d):
        return lax.rem(m + MP - d, MP)

    def ipeer(d):
        return lax.rem(i + d, IN)

    def isource(d):
        return lax.rem(i + IN - d, IN)

    def remote(src, dst, ssem, rsem, axis, dev):
        return pltpu.make_async_remote_copy(
            src_ref=src,
            dst_ref=dst,
            send_sem=ssem,
            recv_sem=rsem,
            device_id={axis: dev},
            device_id_type=MESH,
        )

    barrier = pltpu.get_barrier_semaphore()
    for d in range(1, MP):
        pl.semaphore_signal(barrier, inc=1, device_id={"mp": peer_of(d)}, device_id_type=MESH)
    for d in range(1, IN):
        pl.semaphore_signal(barrier, inc=1, device_id={"inner": ipeer(d)}, device_id_type=MESH)

    loads = []
    for k in range(K):
        loads.append(
            pltpu.make_async_copy(wq.at[:, pl.ds(k * QW, QW)], wq_v.at[k], local_sem.at[k])
        )
    loads.append(pltpu.make_async_copy(wk, wk_v, local_sem.at[K]))
    loads.append(pltpu.make_async_copy(wv, wv_v, local_sem.at[K + 1]))
    loads.append(pltpu.make_async_copy(down.at[0], down_v, local_sem.at[K + 2]))
    loads.append(pltpu.make_async_copy(up.at[0], up_v, local_sem.at[K + 3]))
    loads.append(pltpu.make_async_copy(pool.at[0, :, 0], pool_v, local_sem.at[K + 4]))
    for c in loads:
        c.start()

    pl.semaphore_wait(barrier, MP - 1 + IN - 1)

    sends = []
    for d in range(1, IN):
        c = remote(tokens, x_all.at[i], x_send.at[d], x_recv.at[d], "inner", ipeer(d))
        c.start()
        sends.append(c)
    x_all[i] = tokens[...]

    def side_rows(ref, lo_, width):
        return jnp.concatenate(
            [ref[pl.ds((j * SD + h) * R, R), lo_ : lo_ + width] for j in range(IN)], axis=0
        )

    NT = K * NPAGE
    tab = side_rows(table, 0, NT + 2)
    len_c = tab[:, NT : NT + 1]
    ids_c = tab[:, NT + 1 : NT + 2]
    rows_a = lax.broadcasted_iota(jnp.int32, (RS, RS), 0)
    rows_b = lax.broadcasted_iota(jnp.int32, (RS, RS), 1)
    ids_f = ids_c.astype(f32)
    ids_r = jnp.sum(jnp.where(rows_a == rows_b, ids_f, 0.0), axis=0, keepdims=True)
    same = (ids_f == ids_r) & (rows_a // R == rows_b // R)
    own_iota = lax.broadcasted_iota(jnp.int32, (RS, OC), 1)
    owner_c = jnp.sum(
        jnp.where(own_iota == ids_c, omap[...].astype(f32), 0.0), axis=1, keepdims=True
    )
    owner_r = jnp.sum(jnp.where(rows_a == rows_b, owner_c, 0.0), axis=0, keepdims=True)
    home_c = (lax.broadcasted_iota(jnp.int32, (RS, 1), 0) // R * CAP).astype(f32)
    home_r = (lax.broadcasted_iota(jnp.int32, (1, RS), 1) // R * CAP).astype(f32)
    place_c = home_c + jnp.sum(
        jnp.where(same & (rows_b < rows_a), 1.0, 0.0), axis=1, keepdims=True
    )
    place_r = home_r + jnp.sum(
        jnp.where(same & (rows_a < rows_b), 1.0, 0.0), axis=0, keepdims=True
    )

    for d in range(1, IN):
        remote(tokens, x_all.at[isource(d)], x_send.at[d], x_recv.at[d], "inner", ipeer(d)).wait_recv()
    x = x_all[...].reshape(RS, W)

    q_iota = lax.broadcasted_iota(jnp.int32, (L, RS), 0).astype(f32)
    for dest in range(MP):
        target = (dest * IN + i).astype(f32)
        pick = jnp.where((owner_r == target) & (place_r == q_iota), 1.0, 0.0).astype(bf16)
        lo[dest] = jnp.dot(pick, x, preferred_element_type=f32).astype(bf16)
    for d in range(1, MP):
        c = remote(lo.at[peer_of(d)], lr.at[m], l_send.at[d], l_recv.at[d], "mp", peer_of(d))
        c.start()
        sends.append(c)
    lr[m] = lo[m]

    for k in range(K):
        loads[k].wait()
        y = jnp.dot(x, wq_v[k], preferred_element_type=f32)
        part[k] = y.reshape(MP, B, QW).astype(part.dtype)
        for d in range(1, MP):
            c = remote(
                part.at[k, peer_of(d)], rs_in.at[k, d], r_send.at[k, d], r_recv.at[k, d], "mp", peer_of(d)
            )
            c.start()
            sends.append(c)

    col = lax.broadcasted_iota(jnp.int32, (RS, T), 1)
    for k in range(K):
        live = jnp.zeros((RS, T), f32)
        for p in range(NPAGE):
            slot = tab[:, k * NPAGE + p : k * NPAGE + p + 1]
            first = slot * PAGE
            last = first + jnp.where(slot >= 0, jnp.minimum(PAGE, len_c - p * PAGE), 0)
            live = jnp.where((col >= first) & (col < last), 1.0, live)
        bias[k] = jnp.where(live > 0.0, 0.0, -1e30)

    loads[K + 2].wait()
    loads[K + 3].wait()
    for d in range(1, MP):
        remote(
            lo.at[peer_of(d)], lr.at[source_of(d)], l_send.at[d], l_recv.at[d], "mp", peer_of(d)
        ).wait_recv()
    reduced = jnp.zeros((L, down_v.shape[1]), f32)
    for j in range(MP):
        reduced = reduced + jnp.dot(
            lr[j], down_v[j * W : (j + 1) * W, :], preferred_element_type=f32
        )
    rank_now = rank[0]
    pad = down_v.shape[1]
    kept = lax.broadcasted_iota(jnp.int32, (L, pad), 1) < rank_now
    factor = pad / (8.0 * jnp.full((L, pad), rank_now, jnp.int32).astype(f32))
    shrunk = jnp.where(kept, reduced * factor, 0.0).astype(bf16)
    delta = jnp.dot(shrunk, up_v[...], preferred_element_type=f32).astype(bf16)
    for j in range(IN):
        dl_out[j] = delta[:, j * KC : (j + 1) * KC]
    for d in range(1, IN):
        c = remote(dl_out.at[ipeer(d)], dl_in.at[i], d_send.at[d], d_recv.at[d], "inner", ipeer(d))
        c.start()
        sends.append(c)
    dl_in[i] = dl_out[i]

    for j in range(IN):
        rot[pl.ds(j * R, R), :] = rope[pl.ds((j * SD + h) * R, R), :]
    mine = pl.multiple_of(m * B, B)
    rot_c = rot[pl.ds(mine, B), 0:HEAD_WIDTH]
    rot_s = rot[pl.ds(mine, B), HEAD_WIDTH : 2 * HEAD_WIDTH]

    def turn(u):
        return (u * rot_c + pltpu.roll(u, HEAD_WIDTH // 2, 1) * rot_s).astype(bf16)

    for k in range(K):
        for d in range(1, MP):
            remote(
                part.at[k, peer_of(d)], rs_in.at[k, d], r_send.at[k, d], r_recv.at[k, d], "mp", peer_of(d)
            ).wait_recv()
        for g in range(G):
            cut = slice(g * HEAD_WIDTH, (g + 1) * HEAD_WIDTH)
            total = part[k, m, :, cut].astype(f32)
            for d in range(1, MP):
                total = total + rs_in[k, d, :, cut].astype(f32)
            q_all[k, m, :, cut] = turn(total)
        for d in range(1, MP):
            c = remote(
                q_all.at[k, m], q_all.at[k, m], q_send.at[k, d], q_recv.at[k, d], "mp", peer_of(d)
            )
            c.start()
            sends.append(c)

    loads[K].wait()
    loads[K + 1].wait()
    partkv[:, :, 0:KC] = jnp.dot(x, wk_v[...], preferred_element_type=f32).reshape(MP, B, KC)
    vsum = jnp.dot(x, wv_v[...], preferred_element_type=f32)
    for d in range(1, IN):
        remote(
            dl_out.at[ipeer(d)], dl_in.at[isource(d)], d_send.at[d], d_recv.at[d], "inner", ipeer(d)
        ).wait_recv()
    l_iota = lax.broadcasted_iota(jnp.int32, (RS, L), 1).astype(f32)
    for j in range(IN):
        target = (m * IN + j).astype(f32)
        back = jnp.where((owner_c == target) & (place_c == l_iota), 1.0, 0.0).astype(bf16)
        vsum = vsum + jnp.dot(back, dl_in[j], preferred_element_type=f32)
    partkv[:, :, KC : 2 * KC] = vsum.reshape(MP, B, KC)
    for d in range(1, MP):
        c = remote(
            partkv.at[peer_of(d)], rskv.at[d], kv_send.at[d], kv_recv.at[d], "mp", peer_of(d)
        )
        c.start()
        sends.append(c)

    loads[K + 4].wait()
    lane = lax.broadcasted_iota(jnp.int32, (RS, HEAD_WIDTH), 1)
    for k in range(K):
        for d in range(1, MP):
            remote(
                q_all.at[k, m], q_all.at[k, source_of(d)], q_send.at[k, d], q_recv.at[k, d], "mp", peer_of(d)
            ).wait_recv()
        queries = jnp.concatenate(
            [
                q_all[k, :, :, g * HEAD_WIDTH : (g + 1) * HEAD_WIDTH].reshape(RS, HEAD_WIDTH)
                for g in range(G)
            ],
            axis=0,
        )
        keys = pool_v[k, :, :, 0:HEAD_WIDTH].reshape(T, HEAD_WIDTH)
        values = pool_v[k, :, :, HEAD_WIDTH : 2 * HEAD_WIDTH].reshape(T, HEAD_WIDTH)
        s_buf[...] = lax.dot_general(
            queries, keys, (((1,), (1,)), ((), ())), preferred_element_type=f32
        )
        stat = jnp.zeros((RS, HEAD_WIDTH), f32)
        for g in range(G):
            s = s_buf[g * RS : (g + 1) * RS, :] * scale + bias[k]
            top = jnp.max(s, axis=1, keepdims=True)
            e = jnp.exp(s - top)
            p_buf[g * RS : (g + 1) * RS, :] = e.astype(bf16)
            stat = jnp.where(lane == g, top, stat)
            stat = jnp.where(lane == G + g, jnp.sum(e, axis=1, keepdims=True), stat)
        mixed = jnp.dot(p_buf[...], values, preferred_element_type=f32)
        for g in range(G):
            ao[k, :, :, g * HEAD_WIDTH : (g + 1) * HEAD_WIDTH] = (
                mixed[g * RS : (g + 1) * RS, :].reshape(MP, B, HEAD_WIDTH).astype(ao.dtype)
            )
        st[k] = stat.reshape(MP, B, HEAD_WIDTH)
        for d in range(1, MP):
            c = remote(ao.at[k, peer_of(d)], ain.at[k, d], a_send.at[k, d], a_recv.at[k, d], "mp", peer_of(d))
            c.start()
            sends.append(c)
            c = remote(st.at[k, peer_of(d)], sin.at[k, d], t_send.at[k, d], t_recv.at[k, d], "mp", peer_of(d))
            c.start()
            sends.append(c)

    for d in range(1, MP):
        remote(
            partkv.at[peer_of(d)], rskv.at[d], kv_send.at[d], kv_recv.at[d], "mp", peer_of(d)
        ).wait_recv()
    kv = partkv[m]
    for d in range(1, MP):
        kv = kv + rskv[d]
    fresh_key = []
    fresh_value = []
    for k in range(K):
        key = turn(kv[:, k * HEAD_WIDTH : (k + 1) * HEAD_WIDTH])
        value = kv[:, KC + k * HEAD_WIDTH : KC + (k + 1) * HEAD_WIDTH].astype(bf16)
        new_kv[0, :, 2 * k * HEAD_WIDTH : (2 * k + 1) * HEAD_WIDTH] = key
        new_kv[0, :, (2 * k + 1) * HEAD_WIDTH : (2 * k + 2) * HEAD_WIDTH] = value
        fresh_key.append(key.astype(f32))
        fresh_value.append(value.astype(f32))

    for k in range(K):
        for d in range(1, MP):
            remote(
                ao.at[k, peer_of(d)], ain.at[k, d], a_send.at[k, d], a_recv.at[k, d], "mp", peer_of(d)
            ).wait_recv()
            remote(
                st.at[k, peer_of(d)], sin.at[k, d], t_send.at[k, d], t_recv.at[k, d], "mp", peer_of(d)
            ).wait_recv()
        stats = [st[k, m]] + [sin[k, d] for d in range(1, MP)]
        for g in range(G):
            cut = slice(g * HEAD_WIDTH, (g + 1) * HEAD_WIDTH)
            query = q_all[k, m, :, cut].astype(f32)
            fresh = jnp.sum(query * fresh_key[k], axis=1, keepdims=True) * scale
            top = fresh
            for s in stats:
                top = jnp.maximum(top, s[:, g : g + 1])
            shares = [jnp.exp(s[:, g : g + 1] - top) for s in stats]
            fresh_weight = jnp.exp(fresh - top)
            total = fresh_weight
            for s, share in zip(stats, shares):
                total = total + s[:, G + g : G + g + 1] * share
            out = (fresh_weight / total).astype(bf16).astype(f32) * fresh_value[k]
            out = out + (shares[0] / total) * ao[k, m, :, cut].astype(f32)
            for d in range(1, MP):
                out = out + (shares[d] / total) * ain[k, d, :, cut].astype(f32)
            start = k * QW + g * HEAD_WIDTH
            attended[0, :, start : start + HEAD_WIDTH] = out.astype(bf16)

    for c in sends:
        c.wait_send()


def on_device(
    dims,
    tokens,
    query_weight,
    key_weight,
    value_weight,
    adapter_down_weight,
    adapter_up_weight,
    adapter_rank,
    row_adapter_index,
    owner_device_map,
    lengths,
    page_holder_index,
    page_pool_slot,
    key_value_pool,
):
    MP, IN, SD = dims
    R, W = tokens.shape
    RS = R * IN
    B = RS // MP
    QC = query_weight.shape[1]
    KC = key_weight.shape[1]
    K = KC // HEAD_WIDTH
    QW = QC // K
    G = QW // HEAD_WIDTH
    OC = MP * IN
    CAP = max(2, 2 * R // OC)
    L = IN * CAP
    pad = adapter_down_weight.shape[2]
    delta_columns = adapter_up_weight.shape[2]
    slots = key_value_pool.shape[3]
    T = slots * PAGE
    N = lengths.shape[0]
    bf16 = jnp.bfloat16
    f32 = jnp.float32

    held = jnp.where(page_holder_index == lax.axis_index("mp"), page_pool_slot, -1)
    table = jnp.concatenate(
        [held.reshape(N, K * NPAGE), lengths[:, None], row_adapter_index], axis=1
    )
    half = HEAD_WIDTH // 2
    inv_freq = THETA ** (-(2.0 * jnp.arange(half, dtype=f32)) / HEAD_WIDTH)
    angle = lengths.astype(f32)[:, None] * inv_freq
    cosine, sine = jnp.cos(angle), jnp.sin(angle)
    rope = jnp.concatenate([cosine, cosine, -sine, sine], axis=1)

    vmem = pl.BlockSpec(memory_space=pltpu.VMEM)
    hbm = pl.BlockSpec(memory_space=pl.ANY)
    DMA = pltpu.SemaphoreType.DMA
    return pl.pallas_call(
        functools.partial(kernel, dims),
        out_shape=(
            jax.ShapeDtypeStruct((1, B, QC), bf16),
            jax.ShapeDtypeStruct((1, B, 2 * KC), bf16),
        ),
        in_specs=[
            vmem,
            hbm,
            hbm,
            hbm,
            hbm,
            hbm,
            pl.BlockSpec(memory_space=pltpu.SMEM),
            vmem,
            vmem,
            vmem,
            hbm,
        ],
        out_specs=(vmem, vmem),
        scratch_shapes=[
            pltpu.VMEM((IN, R, W), bf16),
            pltpu.VMEM((MP, L, W), bf16),
            pltpu.VMEM((MP, L, W), bf16),
            pltpu.VMEM((K, W, QW), bf16),
            pltpu.VMEM((W, KC), bf16),
            pltpu.VMEM((W, KC), bf16),
            pltpu.VMEM((MP * W, pad), bf16),
            pltpu.VMEM((pad, delta_columns), bf16),
            pltpu.VMEM((K, slots, PAGE, 2 * HEAD_WIDTH), bf16),
            pltpu.VMEM((K, MP, B, QW), PARTIAL),
            pltpu.VMEM((K, MP, B, QW), PARTIAL),
            pltpu.VMEM((MP, B, 2 * KC), f32),
            pltpu.VMEM((MP, B, 2 * KC), f32),
            pltpu.VMEM((K, MP, B, QW), bf16),
            pltpu.VMEM((K, RS, T), f32),
            pltpu.VMEM((G * RS, T), f32),
            pltpu.VMEM((G * RS, T), bf16),
            pltpu.VMEM((K, MP, B, QW), BACK),
            pltpu.VMEM((K, MP, B, HEAD_WIDTH), f32),
            pltpu.VMEM((K, MP, B, QW), BACK),
            pltpu.VMEM((K, MP, B, HEAD_WIDTH), f32),
            pltpu.VMEM((IN, L, KC), bf16),
            pltpu.VMEM((IN, L, KC), bf16),
            pltpu.VMEM((RS, 2 * HEAD_WIDTH), f32),
            DMA((K + 5,)),
            DMA((IN,)),
            DMA((IN,)),
            DMA((MP,)),
            DMA((MP,)),
            DMA((IN,)),
            DMA((IN,)),
            DMA((MP,)),
            DMA((MP,)),
            DMA((K, MP)),
            DMA((K, MP)),
            DMA((K, MP)),
            DMA((K, MP)),
            DMA((K, MP)),
            DMA((K, MP)),
            DMA((K, MP)),
            DMA((K, MP)),
        ],
        compiler_params=pltpu.CompilerParams(
            collective_id=0, has_side_effects=True, vmem_limit_bytes=56 * 1024 * 1024
        ),
    )(
        tokens,
        query_weight,
        key_weight,
        value_weight,
        adapter_down_weight,
        adapter_up_weight,
        adapter_rank,
        table,
        owner_device_map.reshape(1, OC),
        rope,
        key_value_pool,
    )


def solution(mesh):
    in_specs = (
        P(("groups", "inner", "hst"), "mp"),
        P("mp", "inner"),
        P("mp", "inner"),
        P("mp", "inner"),
        P(("groups", "mp", "inner", "hst"), None, None),
        P(("groups", "mp", "inner", "hst"), None, None),
        P(("groups", "mp", "inner", "hst")),
        P("groups", None),
        P("groups"),
        P("groups"),
        P("groups", "inner", None),
        P("groups", "inner", None),
        P(("groups", "mp"), "inner", "hst", None, None, None),
    )
    out_specs = (P(("groups", "hst"), "mp", "inner"), P(("groups", "hst"), "mp", "inner"))
    dims = (mesh.shape["mp"], mesh.shape["inner"], mesh.shape["hst"])
    return jax.shard_map(
        functools.partial(on_device, dims),
        mesh=mesh,
        in_specs=in_specs,
        out_specs=out_specs,
        check_vma=False,
    )
```
